32 devices in a mesh: dp: 2 (over x), seq: 16 (over z, y, core).
Axes of the slice: x: 2, y: 2, z: 4, core: 2. Of those that a mesh axis runs over, the one named last changes fastest.
Arguments:
- queries: bfloat16 [2, 16, 48, 1536], P('dp', 'seq'), may hold values from -100 to 100
- key_field: bfloat16 [2, 16, 48, 1536], P('dp', 'seq'), may hold values from -7 to 7
- value_field: bfloat16 [2, 16, 48, 1536], P('dp', 'seq'), may hold values from -6 to 6
- out_grad: bfloat16 [2, 16, 48, 1536], P('dp', 'seq'), may hold values from -6 to 6
- out_weight: bfloat16 [1536, 1536], P('seq'), may hold values from -0.15625 to 0.15625
- frame_video: int32 [2, 16], P('dp'), may hold values from 0 to 3, never falling along the last dimension, each value on 1 to 8 neighbouring positions
Outputs:
- mixed_out: bfloat16 [2, 16, 48, 1536], P('dp', 'seq')
- query_grad: bfloat16 [2, 16, 48, 1536], P('dp', 'seq')
- key_grad: bfloat16 [2, 16, 48, 1536], P('dp', 'seq')
- value_grad: bfloat16 [2, 16, 48, 1536], P('dp', 'seq')
- weight_grad: float32 [1536, 1536], P('seq')
The draws below stay inside these ranges and needn't reach their ends.
Inputs may be any that keep to these rules, and one draw needn't show every extreme that they name: `frame_video`: each replica's frames are grouped into whole videos in order: ids never fall, each video has 1 to min(32, 8) frames and one has exactly that many.
All inputs are finite; a program needn't handle non-finite values.
Results may differ from the reference program's by a relative error of at most 0.04.
Values may be sent and summed in bfloat16 or wider, within the bound.
A program may use at most 128 MiB of HBM per device.

```python
import math
import jax
import jax.numpy as jnp
import numpy as np
from jax import lax

HEAD = 128
HEADS = 12
DW = 1536
HD = 1536
FRAMES = 16
SPAN = 48
N_DP = 2


def pair_fields(key):
    shape = (N_DP, FRAMES, SPAN, HEADS, HEAD)
    query_base = jnp.clip(jax.random.normal(jax.random.fold_in(key, 11), shape, jnp.float32), -6.0, 6.0)
    key_base = jnp.clip(jax.random.normal(jax.random.fold_in(key, 12), shape, jnp.float32), -6.0, 6.0)
    return (query_base, key_base)


def draw_queries(key, part):
    query_base, key_base = pair_fields(key)
    query_new = query_base.reshape(N_DP, FRAMES, SPAN, HEADS * HEAD)
    return query_new.astype(jnp.bfloat16)


def draw_key_field(key, part):
    query_base, key_base = pair_fields(key)
    key_new = key_base.reshape(N_DP, FRAMES, SPAN, HEADS * HEAD)
    return key_new.astype(jnp.bfloat16)


def shard_levels(stream_key, dims, shards, low, top_value):
    def one(axis_at, blocks):
        steps = jax.random.uniform(jax.random.fold_in(jax.random.fold_in(stream_key, 6), axis_at), (blocks,), jnp.float32, low / len(shards), top_value / len(shards))
        return jnp.repeat(jnp.exp(steps), dims[axis_at] // blocks).reshape((-1,) + (1,) * (len(dims) - axis_at - 1))

    gain = one(*shards[0])
    for cut in shards[1:]:
        gain = gain * one(*cut)
    return gain


def split_up(amount, total, reach, slope):
    weights = [(1 << 20) // math.isqrt(standing ** slope) + 1 for standing in range(2, amount + 1)]
    surplus, holding = total - reach - (amount - 1), [1] * (amount - 1)
    while surplus > 0:
        movable = [i for i in range(amount - 1) if holding[i] < reach]
        whole, left = sum([weights[i] for i in movable]), surplus
        for i in movable:
            extra = min(reach - holding[i], max(1, left * weights[i] // whole), surplus)
            holding[i] = holding[i] + extra
            surplus = surplus - extra
    return np.array([reach] + holding)


def ragged_sizes(key, count, total, limit, slope):
    if count == 2:
        one = jax.random.randint(key, (), max(1, total - limit), min(limit, total - 1) + 1)
        return jnp.stack([one, total - one])
    tallies = jnp.asarray(split_up(count, total, limit, slope), jnp.int32)
    twos = (count - 1) // 2
    source_of, sink = tallies[1:1 + 2 * twos:2], tallies[2:2 + 2 * twos:2]
    room = jnp.minimum(source_of - 1, limit - sink)
    moved = jax.random.randint(jax.random.fold_in(key, 1), (twos,), 0, 1 << 20) % (room + 1)
    tallies = tallies.at[1:1 + 2 * twos:2].set(source_of - moved).at[2:2 + 2 * twos:2].set(sink + moved)
    return tallies[jax.random.permutation(jax.random.fold_in(key, 2), count)]


def bell_draw(own_key, extent, spread, bound, pieces=(), held_as=jnp.bfloat16):
    values = jax.random.normal(own_key, extent, jnp.float32) * spread
    if len(pieces) > 0:
        values = shard_levels(own_key, extent, pieces, -0.22, 0.18) * values
    return jnp.clip(values, min=-bound, max=bound).astype(held_as)


def setup_inputs(seed: int = 0) -> dict:
    seeds = jax.random.split(jax.random.key(seed), 7)
    return {
        "queries": draw_queries(jax.random.fold_in(seeds[6], 71), 0),
        "key_field": draw_key_field(jax.random.fold_in(seeds[6], 71), 0),
        "value_field": bell_draw(seeds[2], (N_DP, FRAMES, SPAN, HD), 1.0, 6.0, ((0, 2), (1, 16))),
        "out_grad": bell_draw(seeds[3], (N_DP, FRAMES, SPAN, DW), 1.0, 6.0, ((0, 2), (1, 16))),
        "out_weight": bell_draw(seeds[4], (HD, DW), HD ** -0.5, 0.15625, ((0, 16),)),
        "frame_video": jax.vmap(lambda own: jnp.searchsorted(jnp.cumsum(ragged_sizes(own, FRAMES // 4, FRAMES, min(32, FRAMES // 2), 2)), jnp.arange(FRAMES), side="right"))(jax.random.split(seeds[5], N_DP)).reshape((N_DP, FRAMES)).astype(jnp.int32),
    }


def reference(queries, key_field, value_field, out_grad, out_weight, frame_video):
    factor = HEAD ** -0.5
    mixed_list = []
    qgrad_list = []
    kgrad_list = []
    vgrad_list = []
    weight_grad = jnp.zeros((HEADS * HEAD, DW), jnp.float32)
    for replica in range(N_DP):
        query4 = queries[replica].reshape(FRAMES, SPAN, HEADS, HEAD).astype(jnp.float32)
        key4 = key_field[replica].reshape(FRAMES, SPAN, HEADS, HEAD).astype(jnp.float32)
        value4 = value_field[replica].reshape(FRAMES, SPAN, HEADS, HEAD).astype(jnp.float32)
        videos = frame_video[replica]
        allowed = (videos[:, None] == videos[None, :])[None, None]
        logits = jnp.einsum('fphe,gphe->phfg', query4, key4) * factor
        logits = jnp.where(allowed, logits, jnp.float32(-1e30))
        shifted = jnp.exp(logits - jnp.max(logits, axis=-1, keepdims=True))
        probs = shifted / jnp.sum(shifted, axis=-1, keepdims=True)
        probs_low = probs.astype(jnp.bfloat16).astype(jnp.float32)
        mixed = jnp.einsum('phfg,gphe->fphe', probs_low, value4).astype(jnp.bfloat16)
        mixed_flat = mixed.reshape(FRAMES * SPAN, HEADS * HEAD)
        out_flat = jnp.dot(mixed_flat, out_weight, preferred_element_type=jnp.float32).astype(jnp.bfloat16)
        grad_flat = out_grad[replica].reshape(FRAMES * SPAN, DW)
        mixed_grad = lax.dot_general(grad_flat, out_weight, (((1,), (1,)), ((), ())), preferred_element_type=jnp.float32).astype(jnp.bfloat16)
        grad4 = mixed_grad.reshape(FRAMES, SPAN, HEADS, HEAD).astype(jnp.float32)
        value_grad = jnp.einsum('phfg,fphe->gphe', probs_low, grad4).astype(jnp.bfloat16)
        through = jnp.einsum('fphe,gphe->phfg', grad4, value4)
        inner = jnp.einsum('fphe,fphe->phf', grad4, mixed.astype(jnp.float32))[..., None]
        score_grad = (probs * (through - inner)).astype(jnp.bfloat16).astype(jnp.float32)
        query_grad = (jnp.einsum('phfg,gphe->fphe', score_grad, key4) * factor).astype(jnp.bfloat16)
        key_grad = (jnp.einsum('phfg,fphe->gphe', score_grad, query4) * factor).astype(jnp.bfloat16)
        weight_grad = weight_grad + lax.dot_general(mixed_flat, grad_flat, (((0,), (0,)), ((), ())), preferred_element_type=jnp.float32)
        mixed_list.append(out_flat.reshape(FRAMES, SPAN, DW))
        qgrad_list.append(query_grad.reshape(FRAMES, SPAN, HEADS * HEAD))
        kgrad_list.append(key_grad.reshape(FRAMES, SPAN, HEADS * HEAD))
        vgrad_list.append(value_grad.reshape(FRAMES, SPAN, HEADS * HEAD))
    return (jnp.stack(mixed_list), jnp.stack(qgrad_list), jnp.stack(kgrad_list), jnp.stack(vgrad_list), weight_grad)
```

```python
import jax
import jax.numpy as jnp
from jax import lax
from jax.sharding import PartitionSpec as P

HEAD = 128
LOW = jnp.bfloat16


def dot(a, b, dims):
    return lax.dot_general(a, b, dims, preferred_element_type=jnp.float32)


def exchange(blocks):
    return lax.all_to_all(blocks, "seq", split_axis=0, concat_axis=0, tiled=True)


def local(queries, key_field, value_field, out_grad, out_weight, frame_video):
    n = lax.axis_size("seq")
    _, own, span, width = queries.shape
    frames = own * n
    per = span // n
    heads = width // HEAD
    rows = own * per * heads
    part = out_weight.shape[0]
    factor = HEAD ** (-0.5)

    def to_blocks(x):
        return x[0].reshape(own, n, per * heads, HEAD).swapaxes(0, 1).reshape(n, rows, HEAD)

    def to_places(x):
        return (
            x.reshape(frames, per, heads, HEAD)
            .swapaxes(0, 1)
            .reshape(per, frames * heads, HEAD)
        )

    def to_frames(x):
        return x.reshape(per, frames, heads, HEAD).swapaxes(0, 1).reshape(n, rows, HEAD)

    def from_blocks(x):
        return x.reshape(n, own, per, width).swapaxes(0, 1).reshape(1, own, span, width)

    grad_all = lax.all_gather(out_grad[0], "seq", axis=0, tiled=True)
    grad_all = grad_all.reshape(frames * span, out_grad.shape[3])

    spread = exchange(
        jnp.concatenate([to_blocks(x) for x in (queries, key_field, value_field)], axis=1)
    )
    query, key, value = (
        to_places(spread[:, i * rows : (i + 1) * rows]) for i in range(3)
    )

    videos = jnp.repeat(frame_video[0], heads)
    head_of = jnp.tile(jnp.arange(heads, dtype=jnp.int32), frames)
    allowed = (videos[:, None] == videos[None, :]) & (head_of[:, None] == head_of[None, :])
    inside = (((2,), (2,)), ((0,), (0,)))
    onward = (((2,), (1,)), ((0,), (0,)))
    across = (((1,), (1,)), ((0,), (0,)))
    logits = jnp.where(allowed[None], dot(query, key, inside) * factor, jnp.float32(-1e30))
    shifted = jnp.exp(logits - jnp.max(logits, axis=-1, keepdims=True))
    probs = shifted / jnp.sum(shifted, axis=-1, keepdims=True)
    probs_low = probs.astype(LOW)
    mixed = dot(probs_low, value, onward).astype(LOW)

    mixed_frames = to_frames(mixed)
    by_feature = mixed_frames.reshape(frames * per, n, part).swapaxes(0, 1)
    by_feature = jnp.pad(by_feature, ((0, 0), (0, 0), (0, HEAD - part)))
    back = exchange(jnp.concatenate([mixed_frames, by_feature], axis=1))
    mixed_rows = from_blocks(back[:, :rows]).reshape(own * span, width)
    mixed_part = (
        back[:, rows:, :part]
        .reshape(n, frames, per, part)
        .swapaxes(0, 1)
        .reshape(frames * span, part)
    )

    out_weight_later, grad_all = lax.optimization_barrier((out_weight, grad_all))
    weight_all = lax.all_gather(out_weight_later, "seq", axis=0, tiled=True)

    mixed_grad = dot(grad_all, out_weight, (((1,), (1,)), ((), ()))).astype(LOW)
    mixed_grad = (
        mixed_grad.reshape(frames, n, per, part).swapaxes(0, 1).reshape(n, frames * per, part)
    )
    grad = to_places(exchange(mixed_grad).swapaxes(0, 1).reshape(frames, per, width))

    value_grad = dot(probs_low, grad, across).astype(LOW)
    through = dot(grad, value, inside)
    inner = jnp.sum(
        grad.astype(jnp.float32) * mixed.astype(jnp.float32), axis=-1, keepdims=True
    )
    score_grad = (probs * (through - inner)).astype(LOW)
    query_grad = (dot(score_grad, key, onward) * factor).astype(LOW)
    key_grad = (dot(score_grad, query, across) * factor).astype(LOW)
    home = exchange(
        jnp.concatenate([to_frames(x) for x in (query_grad, key_grad, value_grad)], axis=1)
    )
    q_back, k_back, v_back = (
        from_blocks(home[:, i * rows : (i + 1) * rows]) for i in range(3)
    )

    share = dot(mixed_part, grad_all, (((0,), (0,)), ((), ()))).astype(LOW)
    if lax.axis_size("dp") == 2:
        other = lax.ppermute(share, "dp", [(0, 1), (1, 0)])
        weight_grad = share.astype(jnp.float32) + other.astype(jnp.float32)
    else:
        weight_grad = lax.psum(share, "dp").astype(jnp.float32)

    mixed_out = dot(mixed_rows, weight_all, (((1,), (0,)), ((), ()))).astype(LOW)
    return (mixed_out.reshape(out_grad.shape), q_back, k_back, v_back, weight_grad)


def solution(mesh):
    placed = (
        P("dp", "seq", None, None),
        P("dp", "seq", None, None),
        P("dp", "seq", None, None),
        P("dp", "seq", None, None),
        P("seq", None),
        P("dp", None),
    )
    return jax.shard_map(
        local,
        mesh=mesh,
        in_specs=placed,
        out_specs=(
            P("dp", "seq", None, None),
            P("dp", "seq", None, None),
            P("dp", "seq", None, None),
            P("dp", "seq", None, None),
            P("seq", None),
        ),
        check_vma=False,
    )
```

```python
import jax
import jax.numpy as jnp
from jax import lax
from jax.sharding import PartitionSpec as P

HEAD = 128
LOW = jnp.bfloat16


def dot(a, b, dims):
    return lax.dot_general(a, b, dims, preferred_element_type=jnp.float32)


def exchange(blocks):
    return lax.all_to_all(blocks, "seq", split_axis=0, concat_axis=0, tiled=True)


def local(queries, key_field, value_field, out_grad, out_weight, frame_video):
    n = lax.axis_size("seq")
    _, own, span, width = queries.shape
    frames = own * n
    per = span // n
    heads = width // HEAD
    rows = own * per * heads
    part = out_weight.shape[0]
    factor = HEAD ** (-0.5)

    def to_blocks(x):
        return x[0].reshape(own, n, per * heads, HEAD).swapaxes(0, 1).reshape(n, rows, HEAD)

    def to_places(x):
        return (
            x.reshape(frames, per, heads, HEAD)
            .swapaxes(0, 1)
            .reshape(per, frames * heads, HEAD)
        )

    def to_frames(x):
        return x.reshape(per, frames, heads, HEAD).swapaxes(0, 1).reshape(n, rows, HEAD)

    def from_blocks(x):
        return x.reshape(n, own, per, width).swapaxes(0, 1).reshape(1, own, span, width)

    grad_all = lax.all_gather(out_grad[0], "seq", axis=0, tiled=True)
    grad_all = grad_all.reshape(frames * span, out_grad.shape[3])

    spread = exchange(
        jnp.concatenate([to_blocks(x) for x in (queries, key_field, value_field)], axis=1)
    )
    query, key, value = (
        to_places(spread[:, i * rows : (i + 1) * rows]) for i in range(3)
    )

    videos = jnp.repeat(frame_video[0], heads)
    head_of = jnp.tile(jnp.arange(heads, dtype=jnp.int32), frames)
    allowed = (videos[:, None] == videos[None, :]) & (head_of[:, None] == head_of[None, :])
    inside = (((2,), (2,)), ((0,), (0,)))
    onward = (((2,), (1,)), ((0,), (0,)))
    across = (((1,), (1,)), ((0,), (0,)))
    logits = jnp.where(allowed[None], dot(query, key, inside) * factor, jnp.float32(-1e30))
    shifted = jnp.exp(logits - jnp.max(logits, axis=-1, keepdims=True))
    probs = shifted / jnp.sum(shifted, axis=-1, keepdims=True)
    probs_low = probs.astype(LOW)
    mixed = dot(probs_low, value, onward).astype(LOW)

    by_feature = to_frames(mixed).reshape(frames * per, n, part).swapaxes(0, 1)
    mixed_part = (
        exchange(by_feature)
        .reshape(n, frames, per, part)
        .swapaxes(0, 1)
        .reshape(frames * span, part)
    )

    out_terms = dot(mixed_part, out_weight, (((1,), (0,)), ((), ()))).astype(LOW)
    mixed_out = lax.psum_scatter(out_terms, "seq", scatter_dimension=0, tiled=True)
    _, grad_all = lax.optimization_barrier((out_terms, grad_all))

    mixed_grad = dot(grad_all, out_weight, (((1,), (1,)), ((), ()))).astype(LOW)
    mixed_grad = (
        mixed_grad.reshape(frames, n, per, part).swapaxes(0, 1).reshape(n, frames * per, part)
    )
    grad = to_places(exchange(mixed_grad).swapaxes(0, 1).reshape(frames, per, width))

    value_grad = dot(probs_low, grad, across).astype(LOW)
    through = dot(grad, value, inside)
    inner = jnp.sum(
        grad.astype(jnp.float32) * mixed.astype(jnp.float32), axis=-1, keepdims=True
    )
    score_grad = (probs * (through - inner)).astype(LOW)
    query_grad = (dot(score_grad, key, onward) * factor).astype(LOW)
    key_grad = (dot(score_grad, query, across) * factor).astype(LOW)
    home = exchange(
        jnp.concatenate([to_frames(x) for x in (query_grad, key_grad, value_grad)], axis=1)
    )
    q_back, k_back, v_back = (
        from_blocks(home[:, i * rows : (i + 1) * rows]) for i in range(3)
    )

    share = dot(mixed_part, grad_all, (((0,), (0,)), ((), ()))).astype(LOW)
    if lax.axis_size("dp") == 2:
        other = lax.ppermute(share, "dp", [(0, 1), (1, 0)])
        weight_grad = share.astype(jnp.float32) + other.astype(jnp.float32)
    else:
        weight_grad = lax.psum(share, "dp").astype(jnp.float32)

    return (mixed_out.reshape(out_grad.shape), q_back, k_back, v_back, weight_grad)


def solution(mesh):
    placed = (
        P("dp", "seq", None, None),
        P("dp", "seq", None, None),
        P("dp", "seq", None, None),
        P("dp", "seq", None, None),
        P("seq", None),
        P("dp", None),
    )
    return jax.shard_map(
        local,
        mesh=mesh,
        in_specs=placed,
        out_specs=(
            P("dp", "seq", None, None),
            P("dp", "seq", None, None),
            P("dp", "seq", None, None),
            P("dp", "seq", None, None),
            P("seq", None),
        ),
        check_vma=False,
    )
```

```python
import jax
import jax.numpy as jnp
from jax import lax
from jax.sharding import PartitionSpec as P

HEAD = 128
LOW = jnp.bfloat16


def dot(a, b, dims):
    return lax.dot_general(a, b, dims, preferred_element_type=jnp.float32)


def exchange(blocks):
    return lax.all_to_all(blocks, "seq", split_axis=0, concat_axis=0, tiled=True)


def local(queries, key_field, value_field, out_grad, out_weight, frame_video):
    n = lax.axis_size("seq")
    _, own, span, width = queries.shape
    frames = own * n
    per = span // n
    heads = width // HEAD
    rows = own * per * heads
    part = out_weight.shape[0]
    factor = HEAD ** (-0.5)

    def to_blocks(x):
        return x[0].reshape(own, n, per * heads, HEAD).swapaxes(0, 1).reshape(n, rows, HEAD)

    def to_places(x):
        return (
            x.reshape(frames, per, heads, HEAD)
            .swapaxes(0, 1)
            .reshape(per, frames * heads, HEAD)
        )

    def to_frames(x):
        return x.reshape(per, frames, heads, HEAD).swapaxes(0, 1).reshape(n, rows, HEAD)

    def from_blocks(x):
        return x.reshape(n, own, per, width).swapaxes(0, 1).reshape(1, own, span, width)

    grad_all = lax.all_gather(out_grad[0], "seq", axis=0, tiled=True)
    grad_all = grad_all.reshape(frames * span, out_grad.shape[3])

    spread = exchange(
        jnp.concatenate([to_blocks(x) for x in (queries, key_field, value_field)], axis=1)
    )
    query, key, value = (
        to_places(spread[:, i * rows : (i + 1) * rows]) for i in range(3)
    )

    videos = jnp.repeat(frame_video[0], heads)
    head_of = jnp.tile(jnp.arange(heads, dtype=jnp.int32), frames)
    allowed = (videos[:, None] == videos[None, :]) & (head_of[:, None] == head_of[None, :])
    inside = (((2,), (2,)), ((0,), (0,)))
    onward = (((2,), (1,)), ((0,), (0,)))
    across = (((1,), (1,)), ((0,), (0,)))
    logits = jnp.where(allowed[None], dot(query, key, inside) * factor, jnp.float32(-1e30))
    shifted = jnp.exp(logits - jnp.max(logits, axis=-1, keepdims=True))
    probs = shifted / jnp.sum(shifted, axis=-1, keepdims=True)
    probs_low = probs.astype(LOW)
    mixed = dot(probs_low, value, onward).astype(LOW)

    by_feature = to_frames(mixed).reshape(frames * per, n, part).swapaxes(0, 1)
    mixed_part = (
        exchange(by_feature)
        .reshape(n, frames, per, part)
        .swapaxes(0, 1)
        .reshape(frames * span, part)
    )

    place = lax.axis_index("seq")
    pairs = mixed_part.reshape(n // 2, 2, own * span, part)

    def terms(side):
        picked = lax.dynamic_index_in_dim(pairs, side, 1, keepdims=False)
        return dot(picked, out_weight, (((2,), (0,)), ((), ())))

    sent = terms(1 - place % 2).astype(LOW)
    _, grad_all = lax.optimization_barrier((sent, grad_all))
    total = terms(place % 2) + lax.ppermute(
        sent, "seq", [(i, i ^ 1) for i in range(n)]
    ).astype(jnp.float32)
    mixed_grad = dot(grad_all, out_weight, (((1,), (1,)), ((), ()))).astype(LOW)
    total, mixed_grad = lax.optimization_barrier((total, mixed_grad))
    step = 2
    while step < n:
        halves = total.astype(LOW).reshape(n // step // 2, 2, own * span, total.shape[2])
        side = (place // step) % 2
        sent = lax.dynamic_index_in_dim(halves, 1 - side, 1, keepdims=False)
        kept = lax.dynamic_index_in_dim(halves, side, 1, keepdims=False)
        total = kept.astype(jnp.float32) + lax.ppermute(
            sent, "seq", [(i, i ^ step) for i in range(n)]
        ).astype(jnp.float32)
        step = 2 * step
    mixed_out = total.astype(LOW)

    mixed_grad = (
        mixed_grad.reshape(frames, n, per, part).swapaxes(0, 1).reshape(n, frames * per, part)
    )
    grad = to_places(exchange(mixed_grad).swapaxes(0, 1).reshape(frames, per, width))

    value_grad = dot(probs_low, grad, across).astype(LOW)
    through = dot(grad, value, inside)
    inner = jnp.sum(
        grad.astype(jnp.float32) * mixed.astype(jnp.float32), axis=-1, keepdims=True
    )
    score_grad = (probs * (through - inner)).astype(LOW)
    query_grad = (dot(score_grad, key, onward) * factor).astype(LOW)
    key_grad = (dot(score_grad, query, across) * factor).astype(LOW)
    home = exchange(
        jnp.concatenate([to_frames(x) for x in (query_grad, key_grad, value_grad)], axis=1)
    )
    q_back, k_back, v_back = (
        from_blocks(home[:, i * rows : (i + 1) * rows]) for i in range(3)
    )

    share = dot(mixed_part, grad_all, (((0,), (0,)), ((), ()))).astype(LOW)
    if lax.axis_size("dp") == 2:
        other = lax.ppermute(share, "dp", [(0, 1), (1, 0)])
        weight_grad = share.astype(jnp.float32) + other.astype(jnp.float32)
    else:
        weight_grad = lax.psum(share, "dp").astype(jnp.float32)

    return (mixed_out.reshape(out_grad.shape), q_back, k_back, v_back, weight_grad)


def solution(mesh):
    placed = (
        P("dp", "seq", None, None),
        P("dp", "seq", None, None),
        P("dp", "seq", None, None),
        P("dp", "seq", None, None),
        P("seq", None),
        P("dp", None),
    )
    return jax.shard_map(
        local,
        mesh=mesh,
        in_specs=placed,
        out_specs=(
            P("dp", "seq", None, None),
            P("dp", "seq", None, None),
            P("dp", "seq", None, None),
            P("dp", "seq", None, None),
            P("seq", None),
        ),
        check_vma=False,
    )
```

```python
import functools

import jax
import jax.numpy as jnp
from jax import lax
from jax.experimental import pallas as pl
from jax.experimental.pallas import tpu as pltpu
from jax.sharding import PartitionSpec as P

HEAD = 128
LOW = jnp.bfloat16


def dot(a, b, dims):
    return lax.dot_general(a, b, dims, preferred_element_type=jnp.float32)


def exchange_kernel(n, x_ref, o_ref, send_sem, recv_sem, own_sem):
    me = lax.axis_index("seq")
    replica = lax.axis_index("dp")

    def peer(k):
        return lax.rem(me + k, n)

    barrier = pltpu.get_barrier_semaphore()

    def greet(k, carry):
        pl.semaphore_signal(
            barrier, inc=1, device_id=(replica, peer(k)), device_id_type=pl.DeviceIdType.MESH
        )
        return carry

    lax.fori_loop(1, n, greet, 0)
    pl.semaphore_wait(barrier, n - 1)

    def copy(k):
        return pltpu.make_async_remote_copy(
            src_ref=x_ref.at[peer(k)],
            dst_ref=o_ref.at[me],
            send_sem=send_sem.at[k],
            recv_sem=recv_sem.at[k],
            device_id=(replica, peer(k)),
            device_id_type=pl.DeviceIdType.MESH,
        )

    def begin(k, carry):
        copy(k).start()
        return carry

    def finish(k, carry):
        copy(k).wait()
        return carry

    lax.fori_loop(1, n, begin, 0)
    own = pltpu.make_async_copy(x_ref.at[me], o_ref.at[me], own_sem)
    own.start()
    own.wait()
    lax.fori_loop(1, n, finish, 0)


def exchange(blocks, which):
    n, rows, lanes = blocks.shape
    full_rows, full_lanes = -(-rows // 16) * 16, -(-lanes // 128) * 128
    blocks = jnp.pad(blocks, ((0, 0), (0, full_rows - rows), (0, full_lanes - lanes)))
    size = 2 * n * full_rows * full_lanes
    moved = pl.pallas_call(
        functools.partial(exchange_kernel, n),
        out_shape=jax.ShapeDtypeStruct(blocks.shape, blocks.dtype),
        in_specs=[pl.BlockSpec(memory_space=pltpu.VMEM)],
        out_specs=pl.BlockSpec(memory_space=pltpu.VMEM),
        scratch_shapes=[
            pltpu.SemaphoreType.DMA((n,)),
            pltpu.SemaphoreType.DMA((n,)),
            pltpu.SemaphoreType.DMA,
        ],
        compiler_params=pltpu.CompilerParams(
            collective_id=which, has_side_effects=True, vmem_limit_bytes=16 * 1024 * 1024
        ),
        cost_estimate=pl.CostEstimate(
            flops=0, bytes_accessed=64 * size, transcendentals=0
        ),
        name="exchange",
    )(blocks)
    return moved[:, :rows, :lanes]


def local(queries, key_field, value_field, out_grad, out_weight, frame_video):
    n = lax.axis_size("seq")
    _, own, span, width = queries.shape
    frames = own * n
    per = span // n
    heads = width // HEAD
    rows = own * per * heads
    part = out_weight.shape[0]
    factor = HEAD ** (-0.5)

    def to_blocks(x):
        return x[0].reshape(own, n, per * heads, HEAD).swapaxes(0, 1).reshape(n, rows, HEAD)

    def to_places(x):
        return (
            x.reshape(frames, per, heads, HEAD)
            .swapaxes(0, 1)
            .reshape(per, frames * heads, HEAD)
        )

    def to_frames(x):
        return x.reshape(per, frames, heads, HEAD).swapaxes(0, 1).reshape(n, rows, HEAD)

    def from_blocks(x):
        return x.reshape(n, own, per, width).swapaxes(0, 1).reshape(1, own, span, width)

    grad_all = lax.all_gather(out_grad[0], "seq", axis=0, tiled=True)
    grad_all = grad_all.reshape(frames * span, out_grad.shape[3])

    spread = exchange(
        jnp.concatenate([to_blocks(x) for x in (queries, key_field, value_field)], axis=1), 0
    )
    query, key, value = (
        to_places(spread[:, i * rows : (i + 1) * rows]) for i in range(3)
    )

    videos = jnp.repeat(frame_video[0], heads)
    head_of = jnp.tile(jnp.arange(heads, dtype=jnp.int32), frames)
    allowed = (videos[:, None] == videos[None, :]) & (head_of[:, None] == head_of[None, :])
    inside = (((2,), (2,)), ((0,), (0,)))
    onward = (((2,), (1,)), ((0,), (0,)))
    across = (((1,), (1,)), ((0,), (0,)))
    logits = jnp.where(allowed[None], dot(query, key, inside) * factor, jnp.float32(-1e30))
    shifted = jnp.exp(logits - jnp.max(logits, axis=-1, keepdims=True))
    probs = shifted / jnp.sum(shifted, axis=-1, keepdims=True)
    probs_low = probs.astype(LOW)
    mixed = dot(probs_low, value, onward).astype(LOW)

    by_feature = to_frames(mixed).reshape(frames * per, n, part).swapaxes(0, 1)
    mixed_part = (
        exchange(by_feature, 1)
        .reshape(n, frames, per, part)
        .swapaxes(0, 1)
        .reshape(frames * span, part)
    )

    place = lax.axis_index("seq")
    pairs = mixed_part.reshape(n // 2, 2, own * span, part)

    def terms(side):
        picked = lax.dynamic_index_in_dim(pairs, side, 1, keepdims=False)
        return dot(picked, out_weight, (((2,), (0,)), ((), ())))

    sent = terms(1 - place % 2).astype(LOW)
    _, grad_all = lax.optimization_barrier((sent, grad_all))
    total = terms(place % 2) + lax.ppermute(
        sent, "seq", [(i, i ^ 1) for i in range(n)]
    ).astype(jnp.float32)
    mixed_grad = dot(grad_all, out_weight, (((1,), (1,)), ((), ()))).astype(LOW)
    total, mixed_grad = lax.optimization_barrier((total, mixed_grad))
    step = 2
    while step < n:
        halves = total.astype(LOW).reshape(n // step // 2, 2, own * span, total.shape[2])
        side = (place // step) % 2
        sent = lax.dynamic_index_in_dim(halves, 1 - side, 1, keepdims=False)
        kept = lax.dynamic_index_in_dim(halves, side, 1, keepdims=False)
        total = kept.astype(jnp.float32) + lax.ppermute(
            sent, "seq", [(i, i ^ step) for i in range(n)]
        ).astype(jnp.float32)
        step = 2 * step
    mixed_out = total.astype(LOW)

    mixed_grad = (
        mixed_grad.reshape(frames, n, per, part).swapaxes(0, 1).reshape(n, frames * per, part)
    )
    grad = to_places(exchange(mixed_grad, 2).swapaxes(0, 1).reshape(frames, per, width))

    value_grad = dot(probs_low, grad, across).astype(LOW)
    through = dot(grad, value, inside)
    inner = jnp.sum(
        grad.astype(jnp.float32) * mixed.astype(jnp.float32), axis=-1, keepdims=True
    )
    score_grad = (probs * (through - inner)).astype(LOW)
    query_grad = (dot(score_grad, key, onward) * factor).astype(LOW)
    key_grad = (dot(score_grad, query, across) * factor).astype(LOW)
    home = exchange(
        jnp.concatenate([to_frames(x) for x in (query_grad, key_grad, value_grad)], axis=1), 3
    )
    q_back, k_back, v_back = (
        from_blocks(home[:, i * rows : (i + 1) * rows]) for i in range(3)
    )

    share = dot(mixed_part, grad_all, (((0,), (0,)), ((), ()))).astype(LOW)
    if lax.axis_size("dp") == 2:
        other = lax.ppermute(share, "dp", [(0, 1), (1, 0)])
        weight_grad = share.astype(jnp.float32) + other.astype(jnp.float32)
    else:
        weight_grad = lax.psum(share, "dp").astype(jnp.float32)

    return (mixed_out.reshape(out_grad.shape), q_back, k_back, v_back, weight_grad)


def solution(mesh):
    placed = (
        P("dp", "seq", None, None),
        P("dp", "seq", None, None),
        P("dp", "seq", None, None),
        P("dp", "seq", None, None),
        P("seq", None),
        P("dp", None),
    )
    return jax.shard_map(
        local,
        mesh=mesh,
        in_specs=placed,
        out_specs=(
            P("dp", "seq", None, None),
            P("dp", "seq", None, None),
            P("dp", "seq", None, None),
            P("dp", "seq", None, None),
            P("seq", None),
        ),
        check_vma=False,
    )
```

```python
import functools

import jax
import jax.numpy as jnp
from jax import lax
from jax.experimental import pallas as pl
from jax.experimental.pallas import tpu as pltpu
from jax.sharding import PartitionSpec as P

HEAD = 128
LOW = jnp.bfloat16


def dot(a, b, dims):
    return lax.dot_general(a, b, dims, preferred_element_type=jnp.float32)


def exchange_kernel(n, x_ref, o_ref, send_sem, recv_sem, own_sem):
    me = lax.axis_index("seq")
    replica = lax.axis_index("dp")

    def peer(k):
        return lax.rem(me + k, n)

    barrier = pltpu.get_barrier_semaphore()

    def greet(k, carry):
        pl.semaphore_signal(
            barrier, inc=1, device_id=(replica, peer(k)), device_id_type=pl.DeviceIdType.MESH
        )
        return carry

    lax.fori_loop(1, n, greet, 0)
    pl.semaphore_wait(barrier, n - 1)

    def copy(k):
        return pltpu.make_async_remote_copy(
            src_ref=x_ref.at[peer(k)],
            dst_ref=o_ref.at[me],
            send_sem=send_sem.at[k],
            recv_sem=recv_sem.at[k],
            device_id=(replica, peer(k)),
            device_id_type=pl.DeviceIdType.MESH,
        )

    def begin(k, carry):
        copy(k).start()
        return carry

    def finish(k, carry):
        copy(k).wait()
        return carry

    lax.fori_loop(1, n, begin, 0)
    own = pltpu.make_async_copy(x_ref.at[me], o_ref.at[me], own_sem)
    own.start()
    own.wait()
    lax.fori_loop(1, n, finish, 0)


def exchange(blocks, which):
    n, rows, lanes = blocks.shape
    full_rows, full_lanes = -(-rows // 16) * 16, -(-lanes // 128) * 128
    blocks = jnp.pad(blocks, ((0, 0), (0, full_rows - rows), (0, full_lanes - lanes)))
    size = 2 * n * full_rows * full_lanes
    moved = pl.pallas_call(
        functools.partial(exchange_kernel, n),
        out_shape=jax.ShapeDtypeStruct(blocks.shape, blocks.dtype),
        in_specs=[pl.BlockSpec(memory_space=pltpu.VMEM)],
        out_specs=pl.BlockSpec(memory_space=pltpu.VMEM),
        scratch_shapes=[
            pltpu.SemaphoreType.DMA((n,)),
            pltpu.SemaphoreType.DMA((n,)),
            pltpu.SemaphoreType.DMA,
        ],
        compiler_params=pltpu.CompilerParams(
            collective_id=which, has_side_effects=True, vmem_limit_bytes=16 * 1024 * 1024
        ),
        cost_estimate=pl.CostEstimate(
            flops=0, bytes_accessed=64 * size, transcendentals=0
        ),
        name="exchange",
    )(blocks)
    return moved[:, :rows, :lanes]


def local(queries, key_field, value_field, out_grad, out_weight, frame_video):
    n = lax.axis_size("seq")
    _, own, span, width = queries.shape
    frames = own * n
    per = span // n
    heads = width // HEAD
    rows = own * per * heads
    part = out_weight.shape[0]
    factor = HEAD ** (-0.5)

    def to_blocks(x):
        return x[0].reshape(own, n, per * heads, HEAD).swapaxes(0, 1).reshape(n, rows, HEAD)

    def to_places(x):
        return (
            x.reshape(frames, per, heads, HEAD)
            .swapaxes(0, 1)
            .reshape(per, frames * heads, HEAD)
        )

    def to_frames(x):
        return x.reshape(per, frames, heads, HEAD).swapaxes(0, 1).reshape(n, rows, HEAD)

    def from_blocks(x):
        return x.reshape(n, own, per, width).swapaxes(0, 1).reshape(1, own, span, width)

    grad_all = lax.all_gather(out_grad[0], "seq", axis=0, tiled=True)
    grad_all = grad_all.reshape(frames * span, out_grad.shape[3])

    spread = exchange(
        jnp.concatenate([to_blocks(x) for x in (queries, key_field, value_field)], axis=1), 0
    )
    query, key, value = (
        to_places(spread[:, i * rows : (i + 1) * rows]) for i in range(3)
    )

    videos = jnp.repeat(frame_video[0], heads)
    head_of = jnp.tile(jnp.arange(heads, dtype=jnp.int32), frames)
    allowed = (videos[:, None] == videos[None, :]) & (head_of[:, None] == head_of[None, :])
    inside = (((2,), (2,)), ((0,), (0,)))
    onward = (((2,), (1,)), ((0,), (0,)))
    across = (((1,), (1,)), ((0,), (0,)))
    logits = jnp.where(allowed[None], dot(query, key, inside) * factor, jnp.float32(-1e30))
    shifted = jnp.exp(logits - jnp.max(logits, axis=-1, keepdims=True))
    probs = shifted / jnp.sum(shifted, axis=-1, keepdims=True)
    probs_low = probs.astype(LOW)
    mixed = dot(probs_low, value, onward).astype(LOW)

    by_feature = to_frames(mixed).reshape(frames * per, n, part).swapaxes(0, 1)
    mixed_part = (
        exchange(by_feature, 1)
        .reshape(n, frames, per, part)
        .swapaxes(0, 1)
        .reshape(frames * span, part)
    )

    place = lax.axis_index("seq")
    pairs = mixed_part.reshape(n // 2, 2, own * span, part)

    def terms(side):
        picked = lax.dynamic_index_in_dim(pairs, side, 1, keepdims=False)
        return dot(picked, out_weight, (((2,), (0,)), ((), ())))

    def pass_on(sent, step):
        moved = lax.ppermute(sent, "seq", [(i, i ^ step) for i in range(n)])
        return moved.astype(jnp.float32)

    def split(total, step):
        halves = total.astype(LOW).reshape(n // step // 2, 2, own * span, total.shape[2])
        side = (place // step) % 2
        sent = lax.dynamic_index_in_dim(halves, 1 - side, 1, keepdims=False)
        return sent, lax.dynamic_index_in_dim(halves, side, 1, keepdims=False)

    def halve(total, step):
        if step >= n:
            return total
        sent, kept = split(total, step)
        return kept.astype(jnp.float32) + pass_on(sent, step)

    sent = terms(1 - place % 2).astype(LOW)
    _, grad_all = lax.optimization_barrier((sent, grad_all))
    total = terms(place % 2) + pass_on(sent, 1)
    mixed_grad = dot(grad_all, out_weight, (((1,), (1,)), ((), ()))).astype(LOW)
    total, mixed_grad = lax.optimization_barrier((total, mixed_grad))

    mixed_grad = (
        mixed_grad.reshape(frames, n, per, part).swapaxes(0, 1).reshape(n, frames * per, part)
    )
    grad = exchange(mixed_grad, 2)
    total, grad = lax.optimization_barrier((halve(total, 2), grad))
    grad = to_places(grad.swapaxes(0, 1).reshape(frames, per, width))

    value_grad = dot(probs_low, grad, across).astype(LOW)
    through = dot(grad, value, inside)
    inner = jnp.sum(
        grad.astype(jnp.float32) * mixed.astype(jnp.float32), axis=-1, keepdims=True
    )
    score_grad = (probs * (through - inner)).astype(LOW)
    query_grad = (dot(score_grad, key, onward) * factor).astype(LOW)
    key_grad = (dot(score_grad, query, across) * factor).astype(LOW)
    home = jnp.concatenate([to_frames(x) for x in (query_grad, key_grad, value_grad)], axis=1)
    total, home = lax.optimization_barrier((halve(total, 4), home))
    home = exchange(home, 3)
    step = 8
    while step < n:
        total = halve(total, step)
        step = 2 * step
    total, home = lax.optimization_barrier((total, home))
    mixed_out = total.astype(LOW)
    q_back, k_back, v_back = (
        from_blocks(home[:, i * rows : (i + 1) * rows]) for i in range(3)
    )

    share = dot(mixed_part, grad_all, (((0,), (0,)), ((), ()))).astype(LOW)
    if lax.axis_size("dp") == 2:
        other = lax.ppermute(share, "dp", [(0, 1), (1, 0)])
        weight_grad = share.astype(jnp.float32) + other.astype(jnp.float32)
    else:
        weight_grad = lax.psum(share, "dp").astype(jnp.float32)

    return (mixed_out.reshape(out_grad.shape), q_back, k_back, v_back, weight_grad)


def solution(mesh):
    placed = (
        P("dp", "seq", None, None),
        P("dp", "seq", None, None),
        P("dp", "seq", None, None),
        P("dp", "seq", None, None),
        P("seq", None),
        P("dp", None),
    )
    return jax.shard_map(
        local,
        mesh=mesh,
        in_specs=placed,
        out_specs=(
            P("dp", "seq", None, None),
            P("dp", "seq", None, None),
            P("dp", "seq", None, None),
            P("dp", "seq", None, None),
            P("seq", None),
        ),
        check_vma=False,
    )
```

```python
import functools

import jax
import jax.numpy as jnp
from jax import lax
from jax.experimental import pallas as pl
from jax.experimental.pallas import tpu as pltpu
from jax.sharding import PartitionSpec as P

HEAD = 128
LOW = jnp.bfloat16


def dot(a, b, dims):
    return lax.dot_general(a, b, dims, preferred_element_type=jnp.float32)


def exchange_kernel(n, x_ref, o_ref, send_sem, recv_sem, own_sem):
    me = lax.axis_index("seq")
    replica = lax.axis_index("dp")

    def peer(k):
        return lax.rem(me + k, n)

    barrier = pltpu.get_barrier_semaphore()

    def greet(k, carry):
        pl.semaphore_signal(
            barrier, inc=1, device_id=(replica, peer(k)), device_id_type=pl.DeviceIdType.MESH
        )
        return carry

    lax.fori_loop(1, n, greet, 0)
    pl.semaphore_wait(barrier, n - 1)

    def copy(k):
        return pltpu.make_async_remote_copy(
            src_ref=x_ref.at[peer(k)],
            dst_ref=o_ref.at[me],
            send_sem=send_sem.at[k],
            recv_sem=recv_sem.at[k],
            device_id=(replica, peer(k)),
            device_id_type=pl.DeviceIdType.MESH,
        )

    def begin(k, carry):
        copy(k).start()
        return carry

    def finish(k, carry):
        copy(k).wait()
        return carry

    lax.fori_loop(1, n, begin, 0)
    own = pltpu.make_async_copy(x_ref.at[me], o_ref.at[me], own_sem)
    own.start()
    own.wait()
    lax.fori_loop(1, n, finish, 0)


def exchange(blocks, which):
    n, rows, lanes = blocks.shape
    full_rows, full_lanes = -(-rows // 16) * 16, -(-lanes // 128) * 128
    blocks = jnp.pad(blocks, ((0, 0), (0, full_rows - rows), (0, full_lanes - lanes)))
    size = 2 * n * full_rows * full_lanes
    moved = pl.pallas_call(
        functools.partial(exchange_kernel, n),
        out_shape=jax.ShapeDtypeStruct(blocks.shape, blocks.dtype),
        in_specs=[pl.BlockSpec(memory_space=pltpu.VMEM)],
        out_specs=pl.BlockSpec(memory_space=pltpu.VMEM),
        scratch_shapes=[
            pltpu.SemaphoreType.DMA((n,)),
            pltpu.SemaphoreType.DMA((n,)),
            pltpu.SemaphoreType.DMA,
        ],
        compiler_params=pltpu.CompilerParams(
            collective_id=which, has_side_effects=True, vmem_limit_bytes=16 * 1024 * 1024
        ),
        cost_estimate=pl.CostEstimate(
            flops=0, bytes_accessed=64 * size, transcendentals=0
        ),
        name="exchange",
    )(blocks)
    return moved[:, :rows, :lanes]


def swap_kernel(step, x_ref, o_ref, send_sem, recv_sem):
    me = lax.axis_index("seq")
    partner = me + step - 2 * step * lax.rem(lax.div(me, step), 2)
    target = (lax.axis_index("dp"), partner)
    barrier = pltpu.get_barrier_semaphore()
    pl.semaphore_signal(
        barrier, inc=1, device_id=target, device_id_type=pl.DeviceIdType.MESH
    )
    pl.semaphore_wait(barrier, 1)
    copy = pltpu.make_async_remote_copy(
        src_ref=x_ref,
        dst_ref=o_ref,
        send_sem=send_sem,
        recv_sem=recv_sem,
        device_id=target,
        device_id_type=pl.DeviceIdType.MESH,
    )
    copy.start()
    copy.wait()


def swap(block, step, which):
    return pl.pallas_call(
        functools.partial(swap_kernel, step),
        out_shape=jax.ShapeDtypeStruct(block.shape, block.dtype),
        in_specs=[pl.BlockSpec(memory_space=pltpu.VMEM)],
        out_specs=pl.BlockSpec(memory_space=pltpu.VMEM),
        scratch_shapes=[pltpu.SemaphoreType.DMA, pltpu.SemaphoreType.DMA],
        compiler_params=pltpu.CompilerParams(
            collective_id=which, has_side_effects=True, vmem_limit_bytes=40 * 1024 * 1024
        ),
        cost_estimate=pl.CostEstimate(
            flops=0, bytes_accessed=4 * block.size, transcendentals=0
        ),
        name="swap",
    )(block)


def local(queries, key_field, value_field, out_grad, out_weight, frame_video):
    n = lax.axis_size("seq")
    _, own, span, width = queries.shape
    frames = own * n
    per = span // n
    heads = width // HEAD
    rows = own * per * heads
    part = out_weight.shape[0]
    factor = HEAD ** (-0.5)

    def to_blocks(x):
        return x[0].reshape(own, n, per * heads, HEAD).swapaxes(0, 1).reshape(n, rows, HEAD)

    def to_places(x):
        return (
            x.reshape(frames, per, heads, HEAD)
            .swapaxes(0, 1)
            .reshape(per, frames * heads, HEAD)
        )

    def to_frames(x):
        return x.reshape(per, frames, heads, HEAD).swapaxes(0, 1).reshape(n, rows, HEAD)

    def from_blocks(x):
        return x.reshape(n, own, per, width).swapaxes(0, 1).reshape(1, own, span, width)

    grad_all = lax.all_gather(out_grad[0], "seq", axis=0, tiled=True)
    grad_all = grad_all.reshape(frames * span, out_grad.shape[3])

    spread = exchange(
        jnp.concatenate([to_blocks(x) for x in (queries, key_field, value_field)], axis=1), 0
    )
    query, key, value = (
        to_places(spread[:, i * rows : (i + 1) * rows]) for i in range(3)
    )

    videos = jnp.repeat(frame_video[0], heads)
    head_of = jnp.tile(jnp.arange(heads, dtype=jnp.int32), frames)
    allowed = (videos[:, None] == videos[None, :]) & (head_of[:, None] == head_of[None, :])
    inside = (((2,), (2,)), ((0,), (0,)))
    onward = (((2,), (1,)), ((0,), (0,)))
    across = (((1,), (1,)), ((0,), (0,)))
    logits = jnp.where(allowed[None], dot(query, key, inside) * factor, jnp.float32(-1e30))
    shifted = jnp.exp(logits - jnp.max(logits, axis=-1, keepdims=True))
    probs = shifted / jnp.sum(shifted, axis=-1, keepdims=True)
    probs_low = probs.astype(LOW)
    mixed = dot(probs_low, value, onward).astype(LOW)

    by_feature = to_frames(mixed).reshape(frames * per, n, part).swapaxes(0, 1)
    mixed_part = (
        exchange(by_feature, 1)
        .reshape(n, frames, per, part)
        .swapaxes(0, 1)
        .reshape(frames * span, part)
    )

    place = lax.axis_index("seq")
    pairs = mixed_part.reshape(n // 2, 2, own * span, part)

    def terms(side):
        picked = lax.dynamic_index_in_dim(pairs, side, 1, keepdims=False)
        return dot(picked, out_weight, (((2,), (0,)), ((), ())))

    def pass_on(sent, step):
        moved = lax.ppermute(sent, "seq", [(i, i ^ step) for i in range(n)])
        return moved.astype(jnp.float32)

    def split(total, step):
        halves = total.astype(LOW).reshape(n // step // 2, 2, own * span, total.shape[2])
        side = (place // step) % 2
        sent = lax.dynamic_index_in_dim(halves, 1 - side, 1, keepdims=False)
        return sent, lax.dynamic_index_in_dim(halves, side, 1, keepdims=False)

    def halve(total, step):
        if step >= n:
            return total
        sent, kept = split(total, step)
        return kept.astype(jnp.float32) + pass_on(sent, step)

    sent = terms(1 - place % 2).astype(LOW)
    total = terms(place % 2) + pass_on(sent, 1)
    sent, kept = split(total, 2)
    total = kept.astype(jnp.float32) + swap(sent, 2, 4).astype(jnp.float32)
    _, grad_all = lax.optimization_barrier((total, grad_all))
    mixed_grad = dot(grad_all, out_weight, (((1,), (1,)), ((), ()))).astype(LOW)
    total, mixed_grad = lax.optimization_barrier((total, mixed_grad))

    mixed_grad = (
        mixed_grad.reshape(frames, n, per, part).swapaxes(0, 1).reshape(n, frames * per, part)
    )
    grad = exchange(mixed_grad, 2)
    total, grad = lax.optimization_barrier((halve(total, 4), grad))
    grad = to_places(grad.swapaxes(0, 1).reshape(frames, per, width))

    value_grad = dot(probs_low, grad, across).astype(LOW)
    through = dot(grad, value, inside)
    inner = jnp.sum(
        grad.astype(jnp.float32) * mixed.astype(jnp.float32), axis=-1, keepdims=True
    )
    score_grad = (probs * (through - inner)).astype(LOW)
    query_grad = (dot(score_grad, key, onward) * factor).astype(LOW)
    key_grad = (dot(score_grad, query, across) * factor).astype(LOW)
    home = jnp.concatenate([to_frames(x) for x in (query_grad, key_grad, value_grad)], axis=1)
    home = exchange(home, 3)
    step = 8
    while step < n:
        total = halve(total, step)
        step = 2 * step
    total, home = lax.optimization_barrier((total, home))
    mixed_out = total.astype(LOW)
    q_back, k_back, v_back = (
        from_blocks(home[:, i * rows : (i + 1) * rows]) for i in range(3)
    )

    share = dot(mixed_part, grad_all, (((0,), (0,)), ((), ()))).astype(LOW)
    if lax.axis_size("dp") == 2:
        other = lax.ppermute(share, "dp", [(0, 1), (1, 0)])
        weight_grad = share.astype(jnp.float32) + other.astype(jnp.float32)
    else:
        weight_grad = lax.psum(share, "dp").astype(jnp.float32)

    return (mixed_out.reshape(out_grad.shape), q_back, k_back, v_back, weight_grad)


def solution(mesh):
    placed = (
        P("dp", "seq", None, None),
        P("dp", "seq", None, None),
        P("dp", "seq", None, None),
        P("dp", "seq", None, None),
        P("seq", None),
        P("dp", None),
    )
    return jax.shard_map(
        local,
        mesh=mesh,
        in_specs=placed,
        out_specs=(
            P("dp", "seq", None, None),
            P("dp", "seq", None, None),
            P("dp", "seq", None, None),
            P("dp", "seq", None, None),
            P("seq", None),
        ),
        check_vma=False,
    )
```
